32 devices in a mesh: tiles: 8 (over y, x, core), reps: 4 (over z).
Axes of the slice: x: 2, y: 2, z: 4, core: 2. Of those that a mesh axis runs over, the one named last changes fastest.
Arguments:
- tiles_w: bfloat16 [1024, 128, 128], P('tiles'), may hold values from 0.0001 to 4
- tile_worker: int32 [1024], P('tiles'), may hold values from 0 to 15
- tile_owner: int32 [1024], P('tiles'), may hold values from 0 to 7
- owner_block: int32 [8, 8], P('tiles'), may hold values from 0 to 1
- worker_base: float32 [16384], P('tiles'), may hold values from -6 to 6
- worker_noise: float32 [16384], P('tiles'), may hold values from 0.2 to 1.5
- worker_cluster: int32 [16384], P('tiles'), may hold values from 0 to 255
- firm_base: float32 [2048], P('tiles'), may hold values from -6 to 6
- firm_noise: float32 [2048], P('tiles'), may hold values from 0.2 to 1.5
- firm_cluster: int32 [2048], P('tiles'), may hold values from 0 to 255
- signs: int32 [256, 256], P('reps'), may hold values from 0 to 1
- covariates: float32 [2048, 512], P('tiles'), may hold values from -0.125 to 0.125
- whitening: float32 [512, 512], replicated, may hold values from -0.25 to 0.25
Outputs:
- worker_effect: float32 [256, 16384], P('reps', 'tiles')
- firm_effect: float32 [256, 2048], P('reps', 'tiles')
- coefficients: float32 [256, 512], P('reps')
- covariance: float32 [512, 512], P('tiles')
The draws below stay inside these ranges and needn't reach their ends.
Inputs may be any that keep to these rules, and one draw needn't show every extreme that they name: `tile_worker`: local worker block of each tile. `tile_owner`: owner of each tile's firm block. `owner_block`: firm block among the owner's 2 blocks. `signs`: a bit that gives the sign 2 b - 1.
All inputs are finite; a program needn't handle non-finite values.
Results may differ from the reference program's by a relative error of at most 0.0023.
Values may be sent and summed in bfloat16 or wider, within the bound.
A program may use at most 64 MiB of HBM per device.

```python
import math
import jax
import jax.numpy as jnp
import numpy as np
from jax import lax

TILE = 128
TILES_DEV = 128
WORK_BLOCKS = 16
FIRM_BLOCKS = 2
COVARS = 512
CLUSTERS = 256
SWEEPS = 6
TILES = 1024
WORKERS = 16384
FIRMS = 2048
REPLICAS = 256
N_TILES = 8


def draw_tiles_w(key, part):
    tile_shape = (TILES, TILE, TILE)
    key_mask = jax.random.fold_in(key, 701)
    key_strong = jax.random.fold_in(key, 702)
    key_weak = jax.random.fold_in(key, 703)
    resolution = 1 << 20
    cutoff = max(1, min(resolution // 2, 4 * WORK_BLOCKS * resolution // (TILES_DEV * TILE)))
    picked = jax.random.randint(key_mask, tile_shape, 0, resolution) < cutoff
    strong_draw = jax.random.uniform(key_strong, tile_shape, jnp.float32)
    weak_draw = jax.random.uniform(key_weak, tile_shape, jnp.float32)
    weak_value = jnp.exp(jnp.log(0.000101) + weak_draw * (jnp.log(0.02) - jnp.log(0.000101)))
    strong_value = jnp.exp(jnp.log(0.25) + strong_draw * jnp.log(16.0))
    strong_value = jnp.minimum(strong_value, 4.0)
    return jnp.where(picked, strong_value, weak_value).astype(jnp.bfloat16)


def touch_ends(drawn, own_key, smallest, top_value):
    longest = drawn.shape.index(max(drawn.shape))
    spots = []
    for shift in (0, 1):
        where = [jax.random.randint(jax.random.fold_in(own_key, axis), (), 0, length) for axis, length in enumerate(drawn.shape)]
        where[longest] = (where[longest] + shift) % drawn.shape[longest]
        spots.append(tuple(where))
    return drawn.at[spots[0]].set(smallest).at[spots[1]].set(top_value)


def levels(own_key, dims, shards, low, top_value):
    factor_of = 1.0
    for dim, parts in shards:
        steps = jax.random.uniform(jax.random.fold_in(jax.random.fold_in(own_key, 6), dim), (parts,), jnp.float32, low / len(shards), top_value / len(shards))
        factor_of = factor_of * jnp.repeat(jnp.exp(steps), dims[dim] // parts).reshape((-1,) + (1,) * (len(dims) - 1 - dim))
    return factor_of


def rank_table(count, lean):
    loads = [(1 << 20) // math.isqrt(rank ** lean) + 1 for rank in range(1, count + 1)]
    width = 1 + sum(loads) // (1 << 30)
    return np.cumsum(np.array([max(1, weight // width) for weight in loads]))


def ranked_ids(key, dims, count, slope):
    listing = rank_table(count, slope)
    pick = jax.random.randint(jax.random.fold_in(key, 1), dims, 0, int(listing[count - 1]))
    rank = jnp.searchsorted(jnp.asarray(listing, jnp.int32), pick, side="right")
    return jax.random.permutation(jax.random.fold_in(key, 2), count)[rank].astype(jnp.int32)


def noise(stream_key, extent, scale, reach, split=(), kind=jnp.bfloat16):
    entries = jax.random.normal(stream_key, extent, jnp.float32) * scale
    if len(split) > 0:
        entries = levels(stream_key, extent, split, -0.22, 0.18) * entries
    return jnp.clip(entries, min=-reach, max=reach).astype(kind)


def setup_inputs(seed: int = 0) -> dict:
    streams_of = jax.random.split(jax.random.key(seed), 14)
    tiles_w = draw_tiles_w(jax.random.fold_in(streams_of[13], 71), 0)
    tile_worker = touch_ends(ranked_ids(streams_of[1], (TILES,), WORK_BLOCKS, 2), jax.random.fold_in(streams_of[1], 3), 0, WORK_BLOCKS - 1).astype(jnp.int32)
    tile_owner = touch_ends(ranked_ids(streams_of[2], (TILES,), N_TILES, 1), jax.random.fold_in(streams_of[2], 3), 0, N_TILES - 1).astype(jnp.int32)
    owner_block = touch_ends(jax.random.randint(streams_of[3], (N_TILES, N_TILES), 0, FIRM_BLOCKS), jax.random.fold_in(streams_of[3], 1), 0, FIRM_BLOCKS - 1).astype(jnp.int32)
    worker_base = noise(streams_of[4], (WORKERS,), 1.0, 6.0, ((0, 8),), jnp.float32)
    worker_noise = jnp.clip(0.2 + 1.3 * jax.random.uniform(streams_of[5], (WORKERS,), jnp.float32) ** levels(streams_of[5], (WORKERS,), ((0, 8),), -0.2, 0.2), 0.2, 1.5)
    worker_cluster = touch_ends(jax.random.randint(streams_of[6], (WORKERS,), 0, CLUSTERS), jax.random.fold_in(streams_of[6], 1), 0, CLUSTERS - 1).astype(jnp.int32)
    firm_base = noise(streams_of[7], (FIRMS,), 1.0, 6.0, ((0, 8),), jnp.float32)
    firm_noise = jnp.clip(0.2 + 1.3 * jax.random.uniform(streams_of[8], (FIRMS,), jnp.float32) ** levels(streams_of[8], (FIRMS,), ((0, 8),), -0.2, 0.2), 0.2, 1.5)
    firm_cluster = touch_ends(jax.random.randint(streams_of[9], (FIRMS,), 0, CLUSTERS), jax.random.fold_in(streams_of[9], 1), 0, CLUSTERS - 1).astype(jnp.int32)
    signs = touch_ends(jax.random.randint(streams_of[10], (REPLICAS, CLUSTERS), 0, 2), jax.random.fold_in(streams_of[10], 1), 0, 1).astype(jnp.int32)
    covariates = noise(streams_of[11], (FIRMS, COVARS), FIRMS ** -0.5, 0.125, ((0, 8),), jnp.float32)
    whitening = noise(streams_of[12], (COVARS, COVARS), COVARS ** -0.5, 0.25, (), jnp.float32)
    return {"tiles_w": tiles_w, "tile_worker": tile_worker, "tile_owner": tile_owner, "owner_block": owner_block, "worker_base": worker_base, "worker_noise": worker_noise, "worker_cluster": worker_cluster, "firm_base": firm_base, "firm_noise": firm_noise, "firm_cluster": firm_cluster, "signs": signs, "covariates": covariates, "whitening": whitening}


spectral_bound = 0.8


def chebyshev_weights(sweep_count):
    weights = [1.0]
    if sweep_count > 1:
        weights.append(1.0 / (1.0 - 0.5 * spectral_bound * spectral_bound))
    while len(weights) < sweep_count:
        weights.append(1.0 / (1.0 - 0.25 * spectral_bound * spectral_bound * weights[-1]))
    return weights


def reference(tiles_w, tile_worker, tile_owner, owner_block, worker_base, worker_noise, worker_cluster, firm_base, firm_noise, firm_cluster, signs, covariates, whitening):
    highest = lax.Precision.HIGHEST
    owners_count = N_TILES
    worker_total = owners_count * WORK_BLOCKS
    firm_total = owners_count * FIRM_BLOCKS
    tile_groups = tiles_w.reshape(owners_count, TILES_DEV, TILE, TILE)
    owner_grid = tile_owner.reshape(owners_count, TILES_DEV)
    worker_grid = tile_worker.reshape(owners_count, TILES_DEV)
    source_index = jnp.arange(owners_count, dtype=jnp.int32)[:, None]
    block_grid = (owner_grid * FIRM_BLOCKS + owner_block[source_index, owner_grid]).astype(jnp.int32)
    global_workers = (source_index * WORK_BLOCKS + worker_grid).astype(jnp.int32)
    row_mass = jnp.sum(tiles_w, axis=2, dtype=jnp.float32)
    col_mass = jnp.sum(tiles_w, axis=1, dtype=jnp.float32)
    worker_scale = 1.0 + jax.ops.segment_sum(row_mass, global_workers.reshape(-1), num_segments=worker_total)
    firm_scale = 1.0 + jax.ops.segment_sum(col_mass, block_grid.reshape(-1), num_segments=firm_total)
    flip_table = (2 * signs - 1).astype(jnp.float32)
    worker_outcome = worker_base[None, :] + worker_noise[None, :] * flip_table[:, worker_cluster]
    worker_outcome = worker_outcome.reshape(REPLICAS, worker_total, TILE)
    firm_outcome = firm_base[None, :] + firm_noise[None, :] * flip_table[:, firm_cluster]
    firm_outcome = firm_outcome.reshape(REPLICAS, firm_total, TILE)

    def pull(firm_round):
        def per_group(group_data):
            group_tiles, blocks, local_workers = group_data
            tile_firm = jnp.take(firm_round, blocks, axis=1).astype(jnp.float32)
            pulled = jnp.einsum("twf,rtf->rtw", group_tiles.astype(jnp.float32), tile_firm)
            return jax.ops.segment_sum(jnp.transpose(pulled, (1, 0, 2)), local_workers, num_segments=WORK_BLOCKS)
        sums = lax.map(per_group, (tile_groups, block_grid, worker_grid))
        return jnp.transpose(sums, (2, 0, 1, 3)).reshape(REPLICAS, worker_total, TILE)

    def push(worker_round):
        def per_group(carried, group_data):
            group_tiles, blocks, workers_here = group_data
            tile_values = jnp.take(worker_round, workers_here, axis=1).astype(jnp.float32)
            pushed = jnp.einsum("twf,rtw->rtf", group_tiles.astype(jnp.float32), tile_values)
            return carried + jax.ops.segment_sum(jnp.transpose(pushed, (1, 0, 2)), blocks, num_segments=firm_total), None
        start = jnp.zeros((firm_total, REPLICAS, TILE), jnp.float32)
        summed, _ = lax.scan(per_group, start, (tile_groups, block_grid, global_workers))
        return jnp.transpose(summed, (1, 0, 2))

    omegas = chebyshev_weights(SWEEPS)
    firm_older = jnp.zeros((REPLICAS, firm_total, TILE), jnp.float32)
    firm_newer = firm_older
    worker_now = worker_outcome
    firm_now = firm_older
    for sweep_index in range(SWEEPS):
        if sweep_index == 0:
            worker_now = worker_outcome
        else:
            worker_now = worker_outcome - pull(firm_newer.astype(jnp.bfloat16)) / worker_scale[None]
        firm_sum = push(worker_now.astype(jnp.bfloat16))
        firm_target = firm_outcome - firm_sum / firm_scale[None]
        firm_now = firm_older + omegas[sweep_index] * (firm_target - firm_older)
        firm_older, firm_newer = firm_newer, firm_now
    worker_effect = worker_now.reshape(REPLICAS, WORKERS)
    firm_effect = firm_now.reshape(REPLICAS, FIRMS)
    mixing = jnp.dot(covariates, whitening.T, precision=highest)
    coefficients = jnp.dot(firm_effect, mixing, precision=highest)
    covariance = jnp.dot(coefficients.T, coefficients, precision=highest) / REPLICAS
    return worker_effect, firm_effect, coefficients, covariance
```

```python
import functools

import jax
import jax.numpy as jnp
from jax import lax
from jax.experimental import pallas as pl
from jax.experimental.pallas import tpu as pltpu
from jax.sharding import PartitionSpec as P

SWEEPS = 6
WORK_BLOCKS = 16
spectral_bound = 0.8
F32, BF16 = jnp.float32, jnp.bfloat16
NN = (((1,), (0,)), ((), ()))
NT = (((1,), (1,)), ((), ()))
VMEM_BYTES = 60 * 2**20


def chebyshev_weights(sweep_count):
    weights = [1.0]
    weights.append(1.0 / (1.0 - 0.5 * spectral_bound * spectral_bound))
    while len(weights) < sweep_count:
        weights.append(1.0 / (1.0 - 0.25 * spectral_bound * spectral_bound * weights[-1]))
    return weights


def product(a, b, dims=NN):
    return lax.dot_general(a, b, dims, preferred_element_type=F32)


def split(a):
    high = a.astype(BF16)
    return high, (a - high.astype(F32)).astype(BF16)


def fine_product(a, b, dims=NN):
    ah, al = split(a)
    bh, bl = split(b)
    return product(ah, bh, dims) + (product(ah, bl, dims) + product(al, bh, dims))


def dense_kernel(worker_ref, owner_ref, tiles_ref, dense_ref, acc):
    tile_count, cells, _ = tiles_ref.shape
    acc[...] = jnp.zeros_like(acc)

    def add(t, _):
        rows = pl.ds(pl.multiple_of(worker_ref[t] * cells, cells), cells)
        o = owner_ref[t]
        acc[o, rows, :] += tiles_ref[t].astype(F32)
        return 0

    lax.fori_loop(0, tile_count, add, 0)
    for o in range(acc.shape[0]):
        dense_ref[o // 2, :, (o % 2) * cells : (o % 2 + 1) * cells] = acc[o].astype(BF16)


def dense_weights(tiles_w, tile_worker, tile_owner, n):
    cells = tiles_w.shape[1]
    workers = WORK_BLOCKS * cells
    return pl.pallas_call(
        dense_kernel,
        out_shape=jax.ShapeDtypeStruct((n // 2, workers, 2 * cells), BF16),
        in_specs=[
            pl.BlockSpec(memory_space=pltpu.SMEM),
            pl.BlockSpec(memory_space=pltpu.SMEM),
            pl.BlockSpec(memory_space=pltpu.VMEM),
        ],
        out_specs=pl.BlockSpec(memory_space=pltpu.VMEM),
        scratch_shapes=[pltpu.VMEM((n, workers, cells), F32)],
        compiler_params=pltpu.CompilerParams(vmem_limit_bytes=VMEM_BYTES),
    )(tile_worker, tile_owner, tiles_w)


def main_kernel(
    n,
    nz,
    blocks_ref,
    dense_ref,
    wbase_ref,
    wnoise_ref,
    wcluster_ref,
    fbase_ref,
    fnoise_ref,
    fcluster_ref,
    signs_ref,
    cov_ref,
    whit_ref,
    worker_ref,
    firm_ref,
    coef_ref,
    moment_ref,
    outcome,
    wscale,
    foutcome,
    fscale,
    older,
    newer,
    worker_bf,
    pull_sum,
    mixing,
    meta_s,
    meta_r,
    push_s,
    push_r,
    ret_s,
    ret_r,
    part_s,
    part_r,
    sum_s,
    sum_r,
    full,
    mom_s,
    mom_r,
    momsum_s,
    momsum_r,
    sems,
    zsems,
):
    me = lax.axis_index("tiles")
    mz = lax.axis_index("reps")
    chips = n // 2
    chip, core = me // 2, lax.rem(me, 2)
    reps = signs_ref.shape[0]
    cells = push_s.shape[2]
    firm_blocks = foutcome.shape[0]
    barrier = pltpu.get_barrier_semaphore()
    for k in range(1, n):
        pl.semaphore_signal(barrier, inc=1, device_id={"tiles": lax.rem(me + k, n)}, device_id_type=pl.DeviceIdType.MESH)
    for k in range(1, nz):
        pl.semaphore_signal(barrier, inc=1, device_id={"reps": lax.rem(mz + k, nz)}, device_id_type=pl.DeviceIdType.MESH)
    pl.semaphore_wait(barrier, n - 1 + nz - 1)

    def copy(source, target, kind, p):
        return pltpu.make_async_remote_copy(
            src_ref=source.at[p],
            dst_ref=target.at[me],
            send_sem=sems.at[kind, p],
            recv_sem=sems.at[kind + 1, me],
            device_id={"tiles": p},
            device_id_type=pl.DeviceIdType.MESH,
        )

    def finish(source, target, kind, p):
        got = pltpu.make_async_remote_copy(
            src_ref=source.at[p],
            dst_ref=target.at[p],
            send_sem=sems.at[kind, p],
            recv_sem=sems.at[kind + 1, p],
            device_id={"tiles": p},
            device_id_type=pl.DeviceIdType.MESH,
        )
        got.wait_send()
        got.wait_recv()

    def zcopy(source, target, kind, p, at):
        return pltpu.make_async_remote_copy(
            src_ref=source.at[p],
            dst_ref=target.at[at],
            send_sem=zsems.at[kind, p],
            recv_sem=zsems.at[kind + 1, at],
            device_id={"reps": p},
            device_id_type=pl.DeviceIdType.MESH,
        )

    def all_start(source, target, kind):
        for k in range(1, n):
            copy(source, target, kind, lax.rem(me + k, n)).start()

    def all_finish(source, target, kind):
        for k in range(1, n):
            finish(source, target, kind, lax.rem(me + k, n))

    def chip_order(first):
        return [lax.rem(chip + k, chips) for k in (range(chips) if first else list(range(1, chips)) + [0])]

    row = lax.broadcasted_iota(jnp.int32, (8, cells), 0)
    ones_col = jnp.ones((8, dense_ref.shape[1]), BF16)
    for c in range(chips):
        mass = product(ones_col, dense_ref[c])
        for h in range(2):
            o = 2 * c + h
            block = blocks_ref[0:1, o : o + 1].astype(F32)
            meta_s[o] = jnp.where(row == 0, mass[:, h * cells : (h + 1) * cells], block)
    meta_r[me] = meta_s[me]
    all_start(meta_s, meta_r, 0)

    flips = (2 * signs_ref[...] - 1).astype(BF16)

    def wild(base, noise, cluster):
        ids = lax.broadcasted_iota(jnp.int32, (flips.shape[1], cluster.shape[1]), 0)
        hot = jnp.where(ids == cluster, 1.0, 0.0).astype(BF16)
        return base + noise * product(flips, hot)

    step = min(512, wbase_ref.shape[1])
    for at in range(0, wbase_ref.shape[1], step):
        cols = slice(at, at + step)
        value = wild(wbase_ref[:, cols], wnoise_ref[:, cols], wcluster_ref[:, cols])
        outcome[:, cols] = value
        worker_bf[:, cols] = value.astype(BF16)

    def push():
        for c in chip_order(False):
            part = product(worker_bf[...], dense_ref[c]).astype(BF16)
            for h in range(2):
                push_s[2 * c + h] = part[:, h * cells : (h + 1) * cells]

            for h in range(2):
                p = 2 * c + h

                @pl.when(p != me)
                def _():
                    copy(push_s, push_r, 2, p).start()

        push_r[me] = push_s[me]

    push()
    for b in range(firm_blocks):
        cols = slice(b * cells, (b + 1) * cells)
        foutcome[b] = wild(fbase_ref[:, cols], fnoise_ref[:, cols], fcluster_ref[:, cols])
    older[...] = jnp.zeros_like(older)
    newer[...] = jnp.zeros_like(newer)
    ones_row = jnp.ones((8, 2 * cells), BF16)
    degree = product(ones_row, dense_ref[0], NT)
    for c in range(1, chips):
        degree += product(ones_row, dense_ref[c], NT)
    wscale[...] = 1.0 / (1.0 + degree)
    mixing[...] = fine_product(cov_ref[...], whit_ref[...], NT)
    all_finish(meta_s, meta_r, 0)
    for b in range(firm_blocks):
        total = jnp.ones((1, cells), F32)
        for s in range(n):
            total += jnp.where(meta_r[s, 1:2, :] == float(b), meta_r[s, 0:1, :], 0.0)
        fscale[b] = jnp.broadcast_to(1.0 / total, (8, cells))

    def take_push(omega):
        all_finish(push_s, push_r, 2)
        sums = [jnp.zeros((reps, cells), F32) for _ in range(firm_blocks)]
        for s in range(n):
            value = push_r[s].astype(F32)
            block = meta_r[s, 1:2, :]
            for b in range(firm_blocks):
                sums[b] += jnp.where(block == float(b), value, 0.0)
        for b in range(firm_blocks):
            target = foutcome[b] - sums[b] * fscale[b, 0:1, :]
            old = older[b]
            older[b] = newer[b]
            newer[b] = old + omega * (target - old)

    omegas = chebyshev_weights(SWEEPS)

    def sweep(k, _):
        omega = jnp.float32(omegas[0])
        for i in range(1, SWEEPS - 1):
            omega = jnp.where(k == i, jnp.float32(omegas[i]), omega)
        take_push(omega)
        firm = [newer[b] for b in range(firm_blocks)]
        for d in range(1, n + 1):
            p = lax.rem(me + d, n)
            value = firm[0]
            for b in range(1, firm_blocks):
                value = jnp.where(meta_r[p, 1:2, :] == float(b), firm[b], value)
            ret_s[p] = value.astype(BF16)
            if d < n:
                copy(ret_s, ret_r, 4, p).start()
        ret_r[me] = ret_s[me]
        for i, c in enumerate(chip_order(True)):
            for h in range(2):
                p = 2 * c + h

                @pl.when(p != me)
                def _():
                    finish(ret_s, ret_r, 4, p)

            pair = jnp.concatenate([ret_r[2 * c], ret_r[2 * c + 1]], axis=1)
            part = product(pair, dense_ref[c], NT)
            if i == 0:
                pull_sum[...] = part
            else:
                pull_sum[...] += part
        value = outcome[...] - pull_sum[...] * wscale[0:1, :]
        worker_ref[...] = value
        worker_bf[...] = value.astype(BF16)
        push()
        return 0

    lax.fori_loop(0, SWEEPS - 1, sweep, 0)
    take_push(jnp.float32(omegas[SWEEPS - 1]))
    for b in range(firm_blocks):
        firm_ref[:, b * cells : (b + 1) * cells] = newer[b]

    term = fine_product(firm_ref[...], mixing[...])
    share = reps // n
    for p in range(n):
        part_s[p] = term[p * share : (p + 1) * share, :]
    part_r[me] = part_s[me]
    all_start(part_s, part_r, 6)
    all_finish(part_s, part_r, 6)
    total = part_r[0]
    for p in range(1, n):
        total += part_r[p]
    for p in range(n):
        sum_s[p] = total
    sum_r[me] = total
    all_start(sum_s, sum_r, 8)
    all_finish(sum_s, sum_r, 8)
    for p in range(n):
        coef_ref[p * share : (p + 1) * share, :] = sum_r[p]

    coef = coef_ref[...]
    whole = fine_product(coef.T, coef)
    piece = full.shape[1]
    for i in range(n * nz):
        full[i] = whole[i * piece : (i + 1) * piece, :]
    for z in range(nz):
        mom_s[z] = full[me * nz + z]
    mom_r[mz] = mom_s[mz]
    for k in range(1, nz):
        zcopy(mom_s, mom_r, 0, lax.rem(mz + k, nz), mz).start()
    for k in range(1, nz):
        p = lax.rem(mz + k, nz)
        got = zcopy(mom_s, mom_r, 0, p, p)
        got.wait_send()
        got.wait_recv()
    total = mom_r[0]
    for z in range(1, nz):
        total += mom_r[z]
    total = total * (1.0 / (reps * nz))
    for z in range(nz):
        momsum_s[z] = total
    momsum_r[mz] = total
    for k in range(1, nz):
        zcopy(momsum_s, momsum_r, 2, lax.rem(mz + k, nz), mz).start()
    for k in range(1, nz):
        p = lax.rem(mz + k, nz)
        got = zcopy(momsum_s, momsum_r, 2, p, p)
        got.wait_send()
        got.wait_recv()
    for z in range(nz):
        moment_ref[z * piece : (z + 1) * piece, :] = momsum_r[z]


def body(
    tiles_w,
    tile_worker,
    tile_owner,
    owner_block,
    worker_base,
    worker_noise,
    worker_cluster,
    firm_base,
    firm_noise,
    firm_cluster,
    signs,
    covariates,
    whitening,
):
    n, nz = lax.axis_size("tiles"), lax.axis_size("reps")
    cells = tiles_w.shape[1]
    reps = signs.shape[0]
    workers, firms = worker_base.shape[0], firm_base.shape[0]
    blocks = firms // cells
    covars = covariates.shape[1]
    dense = dense_weights(tiles_w, tile_worker, tile_owner, n)
    own = covars // n
    vm = pltpu.VMEM
    return pl.pallas_call(
        functools.partial(main_kernel, n, nz),
        out_shape=(
            jax.ShapeDtypeStruct((reps, workers), F32),
            jax.ShapeDtypeStruct((reps, firms), F32),
            jax.ShapeDtypeStruct((reps, covars), F32),
            jax.ShapeDtypeStruct((own, covars), F32),
        ),
        in_specs=[pl.BlockSpec(memory_space=vm)] * 11,
        out_specs=[pl.BlockSpec(memory_space=vm)] * 4,
        scratch_shapes=[
            vm((reps, workers), F32),
            vm((8, workers), F32),
            vm((blocks, reps, cells), F32),
            vm((blocks, 8, cells), F32),
            vm((blocks, reps, cells), F32),
            vm((blocks, reps, cells), F32),
            vm((reps, workers), BF16),
            vm((reps, workers), F32),
            vm((firms, covars), F32),
            vm((n, 8, cells), F32),
            vm((n, 8, cells), F32),
            vm((n, reps, cells), BF16),
            vm((n, reps, cells), BF16),
            vm((n, reps, cells), BF16),
            vm((n, reps, cells), BF16),
            vm((n, reps // n, covars), F32),
            vm((n, reps // n, covars), F32),
            vm((n, reps // n, covars), F32),
            vm((n, reps // n, covars), F32),
            vm((n * nz, own // nz, covars), F32),
            vm((nz, own // nz, covars), F32),
            vm((nz, own // nz, covars), F32),
            vm((nz, own // nz, covars), F32),
            vm((nz, own // nz, covars), F32),
            pltpu.SemaphoreType.DMA((10, n)),
            pltpu.SemaphoreType.DMA((4, nz)),
        ],
        compiler_params=pltpu.CompilerParams(
            collective_id=0, has_side_effects=True, vmem_limit_bytes=VMEM_BYTES
        ),
    )(
        owner_block,
        dense,
        worker_base[None],
        worker_noise[None],
        worker_cluster[None],
        firm_base[None],
        firm_noise[None],
        firm_cluster[None],
        signs,
        covariates,
        whitening,
    )


def solution(mesh):
    t = P("tiles")
    rows = P("tiles", None)
    placed = (P("tiles", None, None), t, t, rows, t, t, t, t, t, t, P("reps", None), rows, P())
    return jax.shard_map(
        body,
        mesh=mesh,
        in_specs=placed,
        out_specs=(P("reps", "tiles"), P("reps", "tiles"), P("reps", None), P("tiles", None)),
        check_vma=False,
    )
```

```python
import functools

import jax
import jax.numpy as jnp
from jax import lax
from jax.experimental import pallas as pl
from jax.experimental.pallas import tpu as pltpu
from jax.sharding import PartitionSpec as P

SWEEPS = 6
WORK_BLOCKS = 16
spectral_bound = 0.8
F32, BF16 = jnp.float32, jnp.bfloat16
NN = (((1,), (0,)), ((), ()))
NT = (((1,), (1,)), ((), ()))
VMEM_BYTES = 60 * 2**20


def chebyshev_weights(sweep_count):
    weights = [1.0]
    weights.append(1.0 / (1.0 - 0.5 * spectral_bound * spectral_bound))
    while len(weights) < sweep_count:
        weights.append(1.0 / (1.0 - 0.25 * spectral_bound * spectral_bound * weights[-1]))
    return weights


def product(a, b, dims=NN):
    return lax.dot_general(a, b, dims, preferred_element_type=F32)


def split(a):
    high = a.astype(BF16)
    return high, (a - high.astype(F32)).astype(BF16)


def fine_product(a, b, dims=NN):
    ah, al = split(a)
    bh, bl = split(b)
    return product(ah, bh, dims) + (product(ah, bl, dims) + product(al, bh, dims))


def dense_kernel(worker_ref, owner_ref, tiles_ref, dense_ref, acc):
    tile_count, cells, _ = tiles_ref.shape
    acc[...] = jnp.zeros_like(acc)

    def add(t, _):
        rows = pl.ds(pl.multiple_of(worker_ref[t] * cells, cells), cells)
        o = owner_ref[t]
        acc[o, rows, :] += tiles_ref[t].astype(F32)
        return 0

    lax.fori_loop(0, tile_count, add, 0, unroll=8)
    for o in range(acc.shape[0]):
        dense_ref[o // 2, :, (o % 2) * cells : (o % 2 + 1) * cells] = acc[o].astype(BF16)


def dense_weights(tiles_w, tile_worker, tile_owner, n):
    cells = tiles_w.shape[1]
    workers = WORK_BLOCKS * cells
    return pl.pallas_call(
        dense_kernel,
        out_shape=jax.ShapeDtypeStruct((n // 2, workers, 2 * cells), BF16),
        in_specs=[
            pl.BlockSpec(memory_space=pltpu.SMEM),
            pl.BlockSpec(memory_space=pltpu.SMEM),
            pl.BlockSpec(memory_space=pltpu.VMEM),
        ],
        out_specs=pl.BlockSpec(memory_space=pltpu.VMEM),
        scratch_shapes=[pltpu.VMEM((n, workers, cells), F32)],
        compiler_params=pltpu.CompilerParams(
            vmem_limit_bytes=min(VMEM_BYTES, n * workers * cells * 6 + tiles_w.size * 2 + 4 * 2**20)
        ),
    )(tile_worker, tile_owner, tiles_w)


def main_kernel(
    n,
    nz,
    blocks_ref,
    dense_ref,
    wbase_ref,
    wnoise_ref,
    wcluster_ref,
    fbase_ref,
    fnoise_ref,
    fcluster_ref,
    signs_ref,
    cov_ref,
    whit_ref,
    worker_ref,
    firm_ref,
    coef_ref,
    moment_ref,
    outcome,
    wscale,
    foutcome,
    fscale,
    older,
    newer,
    worker_bf,
    pull_sum,
    mixing,
    meta_s,
    meta_r,
    push_s,
    push_r,
    ret_s,
    ret_r,
    part_s,
    part_r,
    sum_s,
    sum_r,
    full,
    mom_s,
    mom_r,
    momsum_s,
    momsum_r,
    sems,
    zsems,
):
    me = lax.axis_index("tiles")
    mz = lax.axis_index("reps")
    chips = n // 2
    chip, core = me // 2, lax.rem(me, 2)
    reps = signs_ref.shape[0]
    cells = push_s.shape[2]
    firm_blocks = foutcome.shape[0]
    barrier = pltpu.get_barrier_semaphore()
    for k in range(1, n):
        pl.semaphore_signal(barrier, inc=1, device_id={"tiles": lax.rem(me + k, n)}, device_id_type=pl.DeviceIdType.MESH)
    for k in range(1, nz):
        pl.semaphore_signal(barrier, inc=1, device_id={"reps": lax.rem(mz + k, nz)}, device_id_type=pl.DeviceIdType.MESH)

    def copy(source, target, kind, p):
        return pltpu.make_async_remote_copy(
            src_ref=source.at[p],
            dst_ref=target.at[me],
            send_sem=sems.at[kind, p],
            recv_sem=sems.at[kind + 1, me],
            device_id={"tiles": p},
            device_id_type=pl.DeviceIdType.MESH,
        )

    def finish(source, target, kind, p):
        got = pltpu.make_async_remote_copy(
            src_ref=source.at[p],
            dst_ref=target.at[p],
            send_sem=sems.at[kind, p],
            recv_sem=sems.at[kind + 1, p],
            device_id={"tiles": p},
            device_id_type=pl.DeviceIdType.MESH,
        )
        return got

    def zcopy(source, target, kind, p, at):
        return pltpu.make_async_remote_copy(
            src_ref=source.at[p],
            dst_ref=target.at[at],
            send_sem=zsems.at[kind, p],
            recv_sem=zsems.at[kind + 1, at],
            device_id={"reps": p},
            device_id_type=pl.DeviceIdType.MESH,
        )

    def all_start(source, target, kind):
        for p in partners(False):
            copy(source, target, kind, p).start()

    def all_finish(source, target, kind):
        for p in partners(True):
            finish(source, target, kind, p).wait_recv()
        all_sent(source, target, kind)

    def all_sent(source, target, kind):
        for p in partners(False):
            finish(source, target, kind, p).wait_send()

    def mate(k):
        if chips & (chips - 1):
            return lax.rem(chip + k, chips)
        other = 0
        for b in (1 << e for e in range(chips.bit_length() - 1)):
            bit = lax.rem(chip // b, 2)
            other = other + b * (1 - bit if k & b else bit)
        return other

    def chip_order(first):
        return [mate(k) for k in (range(chips) if first else range(chips - 1, -1, -1))]

    def partners(near):
        order = [2 * mate(k) + lax.rem(core + h, 2) for k in range(chips) for h in range(2)][1:]
        return order if near else order[::-1]

    row = lax.broadcasted_iota(jnp.int32, (8, cells), 0)
    ones_col = jnp.ones((8, dense_ref.shape[1]), BF16)
    for c in range(chips):
        mass = product(ones_col, dense_ref[c])
        for h in range(2):
            o = 2 * c + h
            block = blocks_ref[0:1, o : o + 1].astype(F32)
            meta_s[o] = jnp.where(row == 0, mass[:, h * cells : (h + 1) * cells], block)

    flips = (2 * signs_ref[...] - 1).astype(BF16)

    def wild(base, noise, cluster):
        ids = lax.broadcasted_iota(jnp.int32, (flips.shape[1], cluster.shape[1]), 0)
        hot = jnp.where(ids == cluster, 1.0, 0.0).astype(BF16)
        return base + noise * product(flips, hot)

    step = min(512, wbase_ref.shape[1])
    for at in range(0, wbase_ref.shape[1], step):
        cols = slice(at, at + step)
        value = wild(wbase_ref[:, cols], wnoise_ref[:, cols], wcluster_ref[:, cols])
        outcome[:, cols] = value
        worker_bf[:, cols] = value.astype(BF16)

    pl.semaphore_wait(barrier, n - 1 + nz - 1)
    meta_r[me] = meta_s[me]
    all_start(meta_s, meta_r, 0)

    def push():
        for c in chip_order(False):
            part = product(worker_bf[...], dense_ref[c]).astype(BF16)
            for h in range(2):
                push_s[2 * c + h] = part[:, h * cells : (h + 1) * cells]

            for h in range(2):
                p = 2 * c + h

                @pl.when(p != me)
                def _():
                    copy(push_s, push_r, 2, p).start()

        push_r[me] = push_s[me]

    push()
    for b in range(firm_blocks):
        cols = slice(b * cells, (b + 1) * cells)
        foutcome[b] = wild(fbase_ref[:, cols], fnoise_ref[:, cols], fcluster_ref[:, cols])
    older[...] = jnp.zeros_like(older)
    newer[...] = jnp.zeros_like(newer)
    ones_row = jnp.ones((8, 2 * cells), BF16)
    degree = product(ones_row, dense_ref[0], NT)
    for c in range(1, chips):
        degree += product(ones_row, dense_ref[c], NT)
    wscale[...] = 1.0 / (1.0 + degree)
    mixing[...] = fine_product(cov_ref[...], whit_ref[...], NT)
    all_finish(meta_s, meta_r, 0)
    for b in range(firm_blocks):
        total = jnp.ones((1, cells), F32)
        for s in range(n):
            total += jnp.where(meta_r[s, 1:2, :] == float(b), meta_r[s, 0:1, :], 0.0)
        fscale[b] = jnp.broadcast_to(1.0 / total, (8, cells))

    def take_push(omega):
        sums = [jnp.zeros((reps, cells), F32) for _ in range(firm_blocks)]
        for s in [me] + partners(True):
            if s is not me:
                finish(push_s, push_r, 2, s).wait_recv()
            value = push_r[s].astype(F32)
            block = meta_r[s, 1:2, :]
            for b in range(firm_blocks):
                sums[b] += jnp.where(block == float(b), value, 0.0)
        for b in range(firm_blocks):
            target = foutcome[b] - sums[b] * fscale[b, 0:1, :]
            old = older[b]
            older[b] = newer[b]
            newer[b] = old + omega * (target - old)

    omegas = chebyshev_weights(SWEEPS)

    def sweep(k, _):
        omega = jnp.float32(omegas[0])
        for i in range(1, SWEEPS - 1):
            omega = jnp.where(k == i, jnp.float32(omegas[i]), omega)
        take_push(omega)
        firm = [newer[b] for b in range(firm_blocks)]
        for p in partners(False) + [me]:
            value = firm[0]
            for b in range(1, firm_blocks):
                value = jnp.where(meta_r[p, 1:2, :] == float(b), firm[b], value)
            ret_s[p] = value.astype(BF16)
            if p is not me:
                copy(ret_s, ret_r, 4, p).start()
        ret_r[me] = ret_s[me]
        all_sent(push_s, push_r, 2)
        for i, c in enumerate(chip_order(True)):
            for h in range(2):
                p = 2 * c + h

                @pl.when(p != me)
                def _():
                    finish(ret_s, ret_r, 4, p).wait_recv()

            pair = jnp.concatenate([ret_r[2 * c], ret_r[2 * c + 1]], axis=1)
            part = product(pair, dense_ref[c], NT)
            if i == 0:
                pull_sum[...] = part
            else:
                pull_sum[...] += part
        value = outcome[...] - pull_sum[...] * wscale[0:1, :]
        worker_ref[...] = value
        worker_bf[...] = value.astype(BF16)
        push()
        all_sent(ret_s, ret_r, 4)
        return 0

    lax.fori_loop(0, SWEEPS - 1, sweep, 0)
    take_push(jnp.float32(omegas[SWEEPS - 1]))
    all_sent(push_s, push_r, 2)
    for b in range(firm_blocks):
        firm_ref[:, b * cells : (b + 1) * cells] = newer[b]

    term = fine_product(firm_ref[...], mixing[...])
    share = reps // n
    for p in range(n):
        part_s[p] = term[p * share : (p + 1) * share, :]
    part_r[me] = part_s[me]
    all_start(part_s, part_r, 6)
    all_finish(part_s, part_r, 6)
    total = part_r[0]
    for p in range(1, n):
        total += part_r[p]
    for p in range(n):
        sum_s[p] = total
    sum_r[me] = total
    all_start(sum_s, sum_r, 8)
    all_finish(sum_s, sum_r, 8)
    for p in range(n):
        coef_ref[p * share : (p + 1) * share, :] = sum_r[p]

    coef = coef_ref[...]
    whole = fine_product(coef.T, coef)
    piece = full.shape[1]
    for i in range(n * nz):
        full[i] = whole[i * piece : (i + 1) * piece, :]
    for z in range(nz):
        mom_s[z] = full[me * nz + z]
    mom_r[mz] = mom_s[mz]
    for k in range(1, nz):
        zcopy(mom_s, mom_r, 0, lax.rem(mz + k, nz), mz).start()
    for k in range(1, nz):
        p = lax.rem(mz + k, nz)
        got = zcopy(mom_s, mom_r, 0, p, p)
        got.wait_send()
        got.wait_recv()
    total = mom_r[0]
    for z in range(1, nz):
        total += mom_r[z]
    total = total * (1.0 / (reps * nz))
    for z in range(nz):
        momsum_s[z] = total
    momsum_r[mz] = total
    for k in range(1, nz):
        zcopy(momsum_s, momsum_r, 2, lax.rem(mz + k, nz), mz).start()
    for k in range(1, nz):
        p = lax.rem(mz + k, nz)
        got = zcopy(momsum_s, momsum_r, 2, p, p)
        got.wait_send()
        got.wait_recv()
    for z in range(nz):
        moment_ref[z * piece : (z + 1) * piece, :] = momsum_r[z]


def emit_kernel(*refs):
    sems = refs[-1]
    half = len(refs) // 2
    copies = [pltpu.make_async_copy(refs[i], refs[half + i], sems.at[i]) for i in range(half)]
    for c in copies:
        c.start()
    for c in copies:
        c.wait()


def emit(results):
    return pl.pallas_call(
        emit_kernel,
        out_shape=tuple(jax.ShapeDtypeStruct(r.shape, r.dtype) for r in results),
        in_specs=[pl.BlockSpec(memory_space=pl.ANY)] * len(results),
        out_specs=[pl.BlockSpec(memory_space=pl.ANY)] * len(results),
        scratch_shapes=[pltpu.SemaphoreType.DMA((len(results),))],
        compiler_params=pltpu.CompilerParams(vmem_limit_bytes=2**20),
    )(*results)


def body(
    tiles_w,
    tile_worker,
    tile_owner,
    owner_block,
    worker_base,
    worker_noise,
    worker_cluster,
    firm_base,
    firm_noise,
    firm_cluster,
    signs,
    covariates,
    whitening,
):
    n, nz = lax.axis_size("tiles"), lax.axis_size("reps")
    cells = tiles_w.shape[1]
    reps = signs.shape[0]
    workers, firms = worker_base.shape[0], firm_base.shape[0]
    blocks = firms // cells
    covars = covariates.shape[1]
    dense = dense_weights(tiles_w, tile_worker, tile_owner, n)
    own = covars // n
    vm = pltpu.VMEM
    results = pl.pallas_call(
        functools.partial(main_kernel, n, nz),
        out_shape=(
            jax.ShapeDtypeStruct((reps, workers), F32),
            jax.ShapeDtypeStruct((reps, firms), F32),
            jax.ShapeDtypeStruct((reps, covars), F32),
            jax.ShapeDtypeStruct((own, covars), F32),
        ),
        in_specs=[pl.BlockSpec(memory_space=vm)] * 11,
        out_specs=[pl.BlockSpec(memory_space=vm)] * 4,
        scratch_shapes=[
            vm((reps, workers), F32),
            vm((8, workers), F32),
            vm((blocks, reps, cells), F32),
            vm((blocks, 8, cells), F32),
            vm((blocks, reps, cells), F32),
            vm((blocks, reps, cells), F32),
            vm((reps, workers), BF16),
            vm((reps, workers), F32),
            vm((firms, covars), F32),
            vm((n, 8, cells), F32),
            vm((n, 8, cells), F32),
            vm((n, reps, cells), BF16),
            vm((n, reps, cells), BF16),
            vm((n, reps, cells), BF16),
            vm((n, reps, cells), BF16),
            vm((n, reps // n, covars), F32),
            vm((n, reps // n, covars), F32),
            vm((n, reps // n, covars), F32),
            vm((n, reps // n, covars), F32),
            vm((n * nz, own // nz, covars), F32),
            vm((nz, own // nz, covars), F32),
            vm((nz, own // nz, covars), F32),
            vm((nz, own // nz, covars), F32),
            vm((nz, own // nz, covars), F32),
            pltpu.SemaphoreType.DMA((10, n)),
            pltpu.SemaphoreType.DMA((4, nz)),
        ],
        compiler_params=pltpu.CompilerParams(
            collective_id=0, has_side_effects=True, vmem_limit_bytes=dense.size * 2 + 20 * 2**20
        ),
    )(
        owner_block,
        dense,
        worker_base[None],
        worker_noise[None],
        worker_cluster[None],
        firm_base[None],
        firm_noise[None],
        firm_cluster[None],
        signs,
        covariates,
        whitening,
    )
    return emit(results)


def solution(mesh):
    t = P("tiles")
    rows = P("tiles", None)
    placed = (P("tiles", None, None), t, t, rows, t, t, t, t, t, t, P("reps", None), rows, P())
    return jax.shard_map(
        body,
        mesh=mesh,
        in_specs=placed,
        out_specs=(P("reps", "tiles"), P("reps", "tiles"), P("reps", None), P("tiles", None)),
        check_vma=False,
    )
```

```python
import functools

import jax
import jax.numpy as jnp
from jax import lax
from jax.experimental import pallas as pl
from jax.experimental.pallas import tpu as pltpu
from jax.sharding import PartitionSpec as P

SWEEPS = 6
WORK_BLOCKS = 16
spectral_bound = 0.8
F32, BF16 = jnp.float32, jnp.bfloat16
NN = (((1,), (0,)), ((), ()))
NT = (((1,), (1,)), ((), ()))
VMEM_BYTES = 60 * 2**20


def chebyshev_weights(sweep_count):
    weights = [1.0]
    weights.append(1.0 / (1.0 - 0.5 * spectral_bound * spectral_bound))
    while len(weights) < sweep_count:
        weights.append(1.0 / (1.0 - 0.25 * spectral_bound * spectral_bound * weights[-1]))
    return weights


def product(a, b, dims=NN):
    return lax.dot_general(a, b, dims, preferred_element_type=F32)


def split(a):
    high = a.astype(BF16)
    return high, (a - high.astype(F32)).astype(BF16)


def fine_product(a, b, dims=NN):
    ah, al = split(a)
    bh, bl = split(b)
    return product(ah, bh, dims) + (product(ah, bl, dims) + product(al, bh, dims))


def dense_kernel(worker_ref, owner_ref, tiles_ref, dense_ref, acc):
    tile_count, cells, _ = tiles_ref.shape
    acc[...] = jnp.zeros_like(acc)

    def add(t, _):
        rows = pl.ds(pl.multiple_of(worker_ref[t] * cells, cells), cells)
        o = owner_ref[t]
        acc[o, rows, :] += tiles_ref[t].astype(F32)
        return 0

    lax.fori_loop(0, tile_count, add, 0, unroll=8)
    for o in range(acc.shape[0]):
        dense_ref[o // 2, :, (o % 2) * cells : (o % 2 + 1) * cells] = acc[o].astype(BF16)


def dense_weights(tiles_w, tile_worker, tile_owner, n):
    cells = tiles_w.shape[1]
    workers = WORK_BLOCKS * cells
    return pl.pallas_call(
        dense_kernel,
        out_shape=jax.ShapeDtypeStruct((n // 2, workers, 2 * cells), BF16),
        in_specs=[
            pl.BlockSpec(memory_space=pltpu.SMEM),
            pl.BlockSpec(memory_space=pltpu.SMEM),
            pl.BlockSpec(memory_space=pltpu.VMEM),
        ],
        out_specs=pl.BlockSpec(memory_space=pltpu.VMEM),
        scratch_shapes=[pltpu.VMEM((n, workers, cells), F32)],
        compiler_params=pltpu.CompilerParams(
            vmem_limit_bytes=min(VMEM_BYTES, n * workers * cells * 6 + tiles_w.size * 2 + 4 * 2**20)
        ),
    )(tile_worker, tile_owner, tiles_w)


def main_kernel(
    n,
    nz,
    blocks_ref,
    dense_ref,
    wbase_ref,
    wnoise_ref,
    wcluster_ref,
    fbase_ref,
    fnoise_ref,
    fcluster_ref,
    signs_ref,
    cov_ref,
    whit_ref,
    worker_ref,
    firm_ref,
    coef_ref,
    moment_ref,
    outcome,
    wscale,
    foutcome,
    fscale,
    older,
    newer,
    worker_bf,
    pull_sum,
    mixing,
    meta_s,
    meta_r,
    push_s,
    push_r,
    ret_s,
    ret_r,
    part_s,
    part_r,
    sum_s,
    sum_r,
    full,
    zall,
    other_s,
    other_r,
    allco,
    sems,
    zsems,
):
    me = lax.axis_index("tiles")
    mz = lax.axis_index("reps")
    chips = n // 2
    chip, core = me // 2, lax.rem(me, 2)
    reps = signs_ref.shape[0]
    cells = push_s.shape[2]
    firm_blocks = foutcome.shape[0]
    barrier = pltpu.get_barrier_semaphore()
    for k in range(1, n):
        pl.semaphore_signal(barrier, inc=1, device_id={"tiles": lax.rem(me + k, n)}, device_id_type=pl.DeviceIdType.MESH)
    for k in range(1, nz):
        pl.semaphore_signal(barrier, inc=1, device_id={"reps": lax.rem(mz + k, nz)}, device_id_type=pl.DeviceIdType.MESH)

    def copy(source, target, kind, p):
        return pltpu.make_async_remote_copy(
            src_ref=source.at[p],
            dst_ref=target.at[me],
            send_sem=sems.at[kind, p],
            recv_sem=sems.at[kind + 1, me],
            device_id={"tiles": p},
            device_id_type=pl.DeviceIdType.MESH,
        )

    def finish(source, target, kind, p):
        got = pltpu.make_async_remote_copy(
            src_ref=source.at[p],
            dst_ref=target.at[p],
            send_sem=sems.at[kind, p],
            recv_sem=sems.at[kind + 1, p],
            device_id={"tiles": p},
            device_id_type=pl.DeviceIdType.MESH,
        )
        return got

    def all_start(source, target, kind):
        for p in partners(False):
            copy(source, target, kind, p).start()

    def all_finish(source, target, kind):
        for p in partners(True):
            finish(source, target, kind, p).wait_recv()
        all_sent(source, target, kind)

    def all_sent(source, target, kind):
        for p in partners(False):
            finish(source, target, kind, p).wait_send()

    def mate(k):
        if chips & (chips - 1):
            return lax.rem(chip + k, chips)
        other = 0
        for b in (1 << e for e in range(chips.bit_length() - 1)):
            bit = lax.rem(chip // b, 2)
            other = other + b * (1 - bit if k & b else bit)
        return other

    def chip_order(first):
        return [mate(k) for k in (range(chips) if first else range(chips - 1, -1, -1))]

    def partners(near):
        order = [2 * mate(k) + lax.rem(core + h, 2) for k in range(chips) for h in range(2)][1:]
        return order if near else order[::-1]

    row = lax.broadcasted_iota(jnp.int32, (8, cells), 0)
    ones_col = jnp.ones((8, dense_ref.shape[1]), BF16)
    for c in range(chips):
        mass = product(ones_col, dense_ref[c])
        for h in range(2):
            o = 2 * c + h
            block = blocks_ref[0:1, o : o + 1].astype(F32)
            meta_s[o] = jnp.where(row == 0, mass[:, h * cells : (h + 1) * cells], block)

    flips = (2 * signs_ref[...] - 1).astype(BF16)

    def wild(base, noise, cluster):
        ids = lax.broadcasted_iota(jnp.int32, (flips.shape[1], cluster.shape[1]), 0)
        hot = jnp.where(ids == cluster, 1.0, 0.0).astype(BF16)
        return base + noise * product(flips, hot)

    step = min(512, wbase_ref.shape[1])
    for at in range(0, wbase_ref.shape[1], step):
        cols = slice(at, at + step)
        value = wild(wbase_ref[:, cols], wnoise_ref[:, cols], wcluster_ref[:, cols])
        outcome[:, cols] = value
        worker_bf[:, cols] = value.astype(BF16)

    pl.semaphore_wait(barrier, n - 1 + nz - 1)
    meta_r[me] = meta_s[me]
    all_start(meta_s, meta_r, 0)

    def push():
        for c in chip_order(False):
            part = product(worker_bf[...], dense_ref[c]).astype(BF16)
            for h in range(2):
                push_s[2 * c + h] = part[:, h * cells : (h + 1) * cells]

            for h in range(2):
                p = 2 * c + h

                @pl.when(p != me)
                def _():
                    copy(push_s, push_r, 2, p).start()

        push_r[me] = push_s[me]

    push()
    for b in range(firm_blocks):
        cols = slice(b * cells, (b + 1) * cells)
        foutcome[b] = wild(fbase_ref[:, cols], fnoise_ref[:, cols], fcluster_ref[:, cols])
    older[...] = jnp.zeros_like(older)
    newer[...] = jnp.zeros_like(newer)
    ones_row = jnp.ones((8, 2 * cells), BF16)
    degree = product(ones_row, dense_ref[0], NT)
    for c in range(1, chips):
        degree += product(ones_row, dense_ref[c], NT)
    wscale[...] = 1.0 / (1.0 + degree)
    mixing[...] = fine_product(cov_ref[...], whit_ref[...], NT)
    all_finish(meta_s, meta_r, 0)
    for b in range(firm_blocks):
        total = jnp.ones((1, cells), F32)
        for s in range(n):
            total += jnp.where(meta_r[s, 1:2, :] == float(b), meta_r[s, 0:1, :], 0.0)
        fscale[b] = jnp.broadcast_to(1.0 / total, (8, cells))

    def take_push(omega):
        sums = [jnp.zeros((reps, cells), F32) for _ in range(firm_blocks)]
        for s in [me] + partners(True):
            if s is not me:
                finish(push_s, push_r, 2, s).wait_recv()
            value = push_r[s].astype(F32)
            block = meta_r[s, 1:2, :]
            for b in range(firm_blocks):
                sums[b] += jnp.where(block == float(b), value, 0.0)
        for b in range(firm_blocks):
            target = foutcome[b] - sums[b] * fscale[b, 0:1, :]
            old = older[b]
            older[b] = newer[b]
            newer[b] = old + omega * (target - old)

    omegas = chebyshev_weights(SWEEPS)

    def sweep(k, _):
        omega = jnp.float32(omegas[0])
        for i in range(1, SWEEPS - 1):
            omega = jnp.where(k == i, jnp.float32(omegas[i]), omega)
        take_push(omega)
        firm = [newer[b] for b in range(firm_blocks)]
        for p in partners(False) + [me]:
            value = firm[0]
            for b in range(1, firm_blocks):
                value = jnp.where(meta_r[p, 1:2, :] == float(b), firm[b], value)
            ret_s[p] = value.astype(BF16)
            if p is not me:
                copy(ret_s, ret_r, 4, p).start()
        ret_r[me] = ret_s[me]
        all_sent(push_s, push_r, 2)
        for i, c in enumerate(chip_order(True)):
            for h in range(2):
                p = 2 * c + h

                @pl.when(p != me)
                def _():
                    finish(ret_s, ret_r, 4, p).wait_recv()

            pair = jnp.concatenate([ret_r[2 * c], ret_r[2 * c + 1]], axis=1)
            part = product(pair, dense_ref[c], NT)
            if i == 0:
                pull_sum[...] = part
            else:
                pull_sum[...] += part
        value = outcome[...] - pull_sum[...] * wscale[0:1, :]
        worker_ref[...] = value
        worker_bf[...] = value.astype(BF16)
        push()
        all_sent(ret_s, ret_r, 4)
        return 0

    lax.fori_loop(0, SWEEPS - 1, sweep, 0)
    take_push(jnp.float32(omegas[SWEEPS - 1]))
    all_sent(push_s, push_r, 2)
    for b in range(firm_blocks):
        firm_ref[:, b * cells : (b + 1) * cells] = newer[b]

    term = fine_product(firm_ref[...], mixing[...])
    share = reps // n
    for p in range(n):
        part_s[p] = term[p * share : (p + 1) * share, :]
    part_r[me] = part_s[me]
    all_start(part_s, part_r, 6)
    all_finish(part_s, part_r, 6)
    total = part_r[0]
    for p in range(1, n):
        total += part_r[p]
    sum_s[...] = total
    for k in range(1, nz):
        pltpu.make_async_remote_copy(
            src_ref=sum_s,
            dst_ref=zall.at[mz],
            send_sem=zsems.at[0, lax.rem(mz + k, nz)],
            recv_sem=zsems.at[1, mz],
            device_id={"reps": lax.rem(mz + k, nz)},
            device_id_type=pl.DeviceIdType.MESH,
        ).start()
    sum_r[me] = total

    def share_copy(kind, source, target, p, at):
        return pltpu.make_async_remote_copy(
            src_ref=source,
            dst_ref=target.at[at],
            send_sem=sems.at[kind, p],
            recv_sem=sems.at[kind + 1, at],
            device_id={"tiles": p},
            device_id_type=pl.DeviceIdType.MESH,
        )

    for p in partners(False):
        share_copy(8, sum_s, sum_r, p, me).start()
    for k in range(1, nz):
        p = lax.rem(mz + k, nz)
        got = pltpu.make_async_remote_copy(
            src_ref=sum_s,
            dst_ref=zall.at[p],
            send_sem=zsems.at[0, p],
            recv_sem=zsems.at[1, p],
            device_id={"reps": p},
            device_id_type=pl.DeviceIdType.MESH,
        )
        got.wait_recv()
        got.wait_send()
        other_s[k - 1] = zall[p]
    other_r[me] = other_s[...]
    for p in partners(False):
        share_copy(10, other_s, other_r, p, me).start()
    for p in partners(True):
        share_copy(8, sum_s, sum_r, p, p).wait_recv()
    for p in range(n):
        coef_ref[p * share : (p + 1) * share, :] = sum_r[p]
        allco[p * share : (p + 1) * share, :] = sum_r[p]
    for p in partners(True):
        share_copy(10, other_s, other_r, p, p).wait_recv()
    for p in range(n):
        for k in range(nz - 1):
            at = reps + (p * (nz - 1) + k) * share
            allco[at : at + share, :] = other_r[p, k]
    for p in partners(True):
        share_copy(8, sum_s, sum_r, p, p).wait_send()
        share_copy(10, other_s, other_r, p, p).wait_send()

    coef = allco[...]
    whole = fine_product(coef.T, coef) * (1.0 / (reps * nz))
    piece = full.shape[1]
    for i in range(n):
        full[i] = whole[i * piece : (i + 1) * piece, :]
    moment_ref[...] = full[me]


def emit_kernel(*refs):
    sems = refs[-1]
    half = len(refs) // 2
    copies = [pltpu.make_async_copy(refs[i], refs[half + i], sems.at[i]) for i in range(half)]
    for c in copies:
        c.start()
    for c in copies:
        c.wait()


def emit(results):
    return pl.pallas_call(
        emit_kernel,
        out_shape=tuple(jax.ShapeDtypeStruct(r.shape, r.dtype) for r in results),
        in_specs=[pl.BlockSpec(memory_space=pl.ANY)] * len(results),
        out_specs=[pl.BlockSpec(memory_space=pl.ANY)] * len(results),
        scratch_shapes=[pltpu.SemaphoreType.DMA((len(results),))],
        compiler_params=pltpu.CompilerParams(vmem_limit_bytes=2**20),
    )(*results)


def body(
    tiles_w,
    tile_worker,
    tile_owner,
    owner_block,
    worker_base,
    worker_noise,
    worker_cluster,
    firm_base,
    firm_noise,
    firm_cluster,
    signs,
    covariates,
    whitening,
):
    n, nz = lax.axis_size("tiles"), lax.axis_size("reps")
    cells = tiles_w.shape[1]
    reps = signs.shape[0]
    workers, firms = worker_base.shape[0], firm_base.shape[0]
    blocks = firms // cells
    covars = covariates.shape[1]
    dense = dense_weights(tiles_w, tile_worker, tile_owner, n)
    own = covars // n
    vm = pltpu.VMEM
    results = pl.pallas_call(
        functools.partial(main_kernel, n, nz),
        out_shape=(
            jax.ShapeDtypeStruct((reps, workers), F32),
            jax.ShapeDtypeStruct((reps, firms), F32),
            jax.ShapeDtypeStruct((reps, covars), F32),
            jax.ShapeDtypeStruct((own, covars), F32),
        ),
        in_specs=[pl.BlockSpec(memory_space=vm)] * 11,
        out_specs=[pl.BlockSpec(memory_space=vm)] * 4,
        scratch_shapes=[
            vm((reps, workers), F32),
            vm((8, workers), F32),
            vm((blocks, reps, cells), F32),
            vm((blocks, 8, cells), F32),
            vm((blocks, reps, cells), F32),
            vm((blocks, reps, cells), F32),
            vm((reps, workers), BF16),
            vm((reps, workers), F32),
            vm((firms, covars), F32),
            vm((n, 8, cells), F32),
            vm((n, 8, cells), F32),
            vm((n, reps, cells), BF16),
            vm((n, reps, cells), BF16),
            vm((n, reps, cells), BF16),
            vm((n, reps, cells), BF16),
            vm((n, reps // n, covars), F32),
            vm((n, reps // n, covars), F32),
            vm((reps // n, covars), F32),
            vm((n, reps // n, covars), F32),
            vm((n, own, covars), F32),
            vm((nz, reps // n, covars), F32),
            vm((nz - 1, reps // n, covars), F32),
            vm((n, nz - 1, reps // n, covars), F32),
            vm((reps * nz, covars), F32),
            pltpu.SemaphoreType.DMA((12, n)),
            pltpu.SemaphoreType.DMA((2, nz)),
        ],
        compiler_params=pltpu.CompilerParams(
            collective_id=0, has_side_effects=True, vmem_limit_bytes=dense.size * 2 + 20 * 2**20
        ),
    )(
        owner_block,
        dense,
        worker_base[None],
        worker_noise[None],
        worker_cluster[None],
        firm_base[None],
        firm_noise[None],
        firm_cluster[None],
        signs,
        covariates,
        whitening,
    )
    return emit(results)


def solution(mesh):
    t = P("tiles")
    rows = P("tiles", None)
    placed = (P("tiles", None, None), t, t, rows, t, t, t, t, t, t, P("reps", None), rows, P())
    return jax.shard_map(
        body,
        mesh=mesh,
        in_specs=placed,
        out_specs=(P("reps", "tiles"), P("reps", "tiles"), P("reps", None), P("tiles", None)),
        check_vma=False,
    )
```
